32 devices in a mesh: pb: 4 (over y, core), kv: 8 (over z, x).
Axes of the slice: x: 2, y: 2, z: 4, core: 2. Of those that a mesh axis runs over, the one named last changes fastest.
Arguments:
- queries: bfloat16 [8192, 4096], P(('pb', 'kv')), may hold values from -6 to 6
- keys: bfloat16 [1024, 4096], P(('pb', 'kv')), may hold values from -6 to 6
- values: bfloat16 [1024, 4096], P(('pb', 'kv')), may hold values from -6 to 6
- key_lists: int32 [64, 8], P('pb'), may hold values from 0 to 7, as said below
- counts: int32 [64], P('pb'), may hold values from 1 to 8, as said below
Outputs:
- attended: bfloat16 [8192, 4096], P(('pb', 'kv'))
The draws below stay inside these ranges and needn't reach their ends.
Inputs may be any that keep to these rules, and one draw needn't show every extreme that they name: For every query block the first counts entries of its row of key_lists name different key blocks; entries past counts are valid block numbers that do not take part. `counts`: some query block uses all 8 entries of its list.
All inputs are finite; a program needn't handle non-finite values.
Results may differ from the reference program's by a relative error of at most 0.011.
Values may be sent and summed in bfloat16 or wider, within the bound.
A program may use at most 64 MiB of HBM per device.

```python
import jax
import jax.numpy as jnp
from jax import lax

HEADS = 32
HD = 128
BLK = 128
MOST = 8
QB_PB = 16
NQB = 64
NQ = 8192
NK = 1024
NKB = 8
WIDTH = 4096


def draw_queries(key, part):
    base = jax.random.fold_in(key, 11)
    field = jax.random.truncated_normal(base, -6.0, 6.0, (NQ, HEADS, HD), jnp.float32)
    return field.reshape(NQ, HEADS * HD).astype(jnp.bfloat16)


def draw_keys(key, part):
    base = jax.random.fold_in(key, 13)
    field = jax.random.truncated_normal(base, -6.0, 6.0, (NK, HEADS, HD), jnp.float32)
    return field.reshape(NK, HEADS * HD).astype(jnp.bfloat16)


def draw_key_lists(key, part):
    row_keys = jax.random.split(jax.random.fold_in(key, 17), NQB)
    chosen = jax.vmap(lambda row_key: jax.random.permutation(row_key, NKB)[:MOST])(row_keys)
    return chosen.astype(jnp.int32)


def draw_counts(key, part):
    first_key, second_key, third_key = jax.random.split(jax.random.fold_in(key, 19), 3)
    ceiling = jax.random.randint(first_key, (NQB // QB_PB,), 2, MOST + 1)
    ceiling_rows = jnp.repeat(ceiling, QB_PB)
    drawn = jax.random.randint(second_key, (NQB,), 0, 1048576) % ceiling_rows + 1
    fullest = jax.random.randint(third_key, (), 0, NQB)
    result = jnp.where(jnp.arange(NQB) == fullest, MOST, drawn)
    return result.astype(jnp.int32)


def block_levels(stream_key, shape, cuts, least, high):
    level, own = 1.0, jax.random.fold_in(stream_key, 6)
    for dim, parts in cuts:
        draws = jnp.exp(jax.random.uniform(jax.random.fold_in(own, dim), (parts,), jnp.float32, least / len(cuts), high / len(cuts)))
        level = level * jnp.repeat(draws, shape[dim] // parts).reshape([-1 if axis == dim else 1 for axis in range(len(shape))])
    return level


def scatter_about(rng, dims, width, bound, shards=(), dtype=jnp.bfloat16):
    values = jax.random.normal(rng, dims, jnp.float32) * width
    if len(shards) > 0:
        values = block_levels(rng, dims, shards, -0.22, 0.18) * values
    return jnp.clip(values, min=-bound, max=bound).astype(dtype)


def setup_inputs(seed: int = 0) -> dict:
    key_list = jax.random.split(jax.random.key(seed), 6)
    queries = draw_queries(jax.random.fold_in(key_list[5], 71), 0)
    keys = draw_keys(jax.random.fold_in(key_list[5], 71), 0)
    values = scatter_about(key_list[2], (NK, WIDTH), 1.0, 6.0, ((0, 32),))
    key_lists = draw_key_lists(jax.random.fold_in(key_list[5], 71), 0)
    counts = draw_counts(jax.random.fold_in(key_list[5], 71), 0)
    return {"queries": queries, "keys": keys, "values": values, "key_lists": key_lists, "counts": counts}


def reference(queries, keys, values, key_lists, counts):
    scaling = HD ** -0.5
    query_blocks = queries.reshape(NQB, BLK, HEADS, HD)
    key_blocks = keys.reshape(NKB, BLK, HEADS, HD)
    value_blocks = values.reshape(NKB, BLK, HEADS, HD)
    slot_of_key = jnp.arange(MOST * BLK) // BLK

    def single(item):
        block_queries, block_list, block_count = item
        listed_keys = key_blocks[block_list].reshape(MOST * BLK, HEADS, HD).astype(jnp.float32)
        listed_values = value_blocks[block_list].reshape(MOST * BLK, HEADS, HD).astype(jnp.float32)
        scores = jnp.einsum("qhd,khd->hqk", block_queries.astype(jnp.float32), listed_keys) * scaling
        usable = slot_of_key < block_count
        largest = jnp.max(jnp.where(usable, scores, -jnp.inf), axis=-1, keepdims=True)
        raised = jnp.where(usable, jnp.exp(scores - largest), 0.0)
        totals = jnp.sum(raised, axis=-1, keepdims=True)
        weights = (raised / totals).astype(jnp.bfloat16)
        output = jnp.einsum("hqk,khd->qhd", weights.astype(jnp.float32), listed_values)
        return output.astype(jnp.bfloat16).reshape(BLK, HEADS * HD)

    produced = lax.map(single, (query_blocks, key_lists, counts))
    return produced.reshape(NQ, HEADS * HD)
```

```python
import functools
import math

import jax
import jax.numpy as jnp
import numpy as np
from jax import lax
from jax.experimental import pallas as pl
from jax.experimental.pallas import tpu as pltpu
from jax.sharding import PartitionSpec as P

HEADS = 32
HD = 128
BLK = 128
MOST = 8

NX, NY, NZ = 2, 2, 4
CHIPS = NX * NY * NZ
HALF = HEADS // 2 * HD
CLASSES = 4
ROUNDS = HEADS // 2 // CLASSES
ROUND_COLS = CLASSES * HD
MESH = pl.DeviceIdType.MESH
FACTOR = HD ** (-0.5) * math.log2(math.e)


def gather_kernel(
    rows_each, q_rows, q_ref, k_ref, v_ref, bias_ref, out_ref,
    kv_buf, q_buf, bias_buf, o_buf,
    recv_sem, send_sem, load_sem, swap_send, swap_recv, out_sem, out_send, out_recv,
):
    pb, kv = lax.axis_index("pb"), lax.axis_index("kv")
    y, core = pb // 2, pb % 2
    z, x = kv // 2, kv % 2
    other = 1 - core
    sibling = (y * 2 + other, kv)
    x_next = (pb, z * 2 + (1 - x))
    y_next = ((1 - y) * 2 + core, kv)
    z_up = (pb, kv + 2)
    z_down = (pb, kv - 2)
    has_up, has_down = z < NZ - 1, z > 0

    barrier = pltpu.get_barrier_semaphore()

    def greet(device):
        pl.semaphore_signal(barrier, inc=1, device_id=device, device_id_type=MESH)

    greet(sibling)
    greet(x_next)
    greet(y_next)

    @pl.when(has_up)
    def _():
        greet(z_up)

    @pl.when(has_down)
    def _():
        greet(z_down)

    def slot_at(cx, cy, cz):
        return (cy * NZ + cz) * NX + cx

    own = slot_at(x, y, z)
    mine = pl.ds(pl.multiple_of(core * HALF, HALF), HALF)
    theirs = pl.ds(pl.multiple_of(other * HALF, HALF), HALF)
    tokens = pl.ds(pl.multiple_of(core * rows_each, rows_each), rows_each)
    q_mine = pl.ds(pl.multiple_of(core * q_rows, q_rows), q_rows)
    q_theirs = pl.ds(pl.multiple_of(other * q_rows, q_rows), q_rows)
    pairs = [
        (k_ref, kv_buf.at[own, 0, tokens, :]),
        (v_ref, kv_buf.at[own, 1, tokens, :]),
        (q_ref, q_buf.at[q_mine, :]),
    ]
    locals_ = [
        pltpu.make_async_copy(source.at[:, mine], target, load_sem.at[i])
        for i, (source, target) in enumerate(pairs)
    ]
    locals_.append(pltpu.make_async_copy(bias_ref, bias_buf.at[core], load_sem.at[3]))
    for copy in locals_:
        copy.start()

    pl.semaphore_wait(barrier, 3 + has_up.astype(jnp.int32) + has_down.astype(jnp.int32))

    def swap(source, target, i):
        return pltpu.make_async_remote_copy(
            src_ref=source, dst_ref=target, send_sem=swap_send.at[i], recv_sem=swap_recv.at[i],
            device_id=sibling, device_id_type=MESH,
        )

    swaps = [swap(source.at[:, theirs], target, i) for i, (source, target) in enumerate(pairs)]
    swaps.append(swap(bias_ref, bias_buf.at[core], 3))
    for copy in swaps:
        copy.start()
    for i in range(2):
        locals_[i].wait()
        swaps[i].wait_recv()

    kinds = [("z", "x"), ("z", "y"), ("a", "x"), ("a", "y")]

    def columns(r, cl):
        return pl.ds(pl.multiple_of(r * ROUND_COLS + cl * HD, HD), HD)

    def place(cl, a, b, cz):
        a_axis = kinds[cl][1]
        dx, dy = (a, b) if a_axis == "x" else (b, a)
        return slot_at(1 - x if dx else x, 1 - y if dy else y, cz)

    def copy_of(r, cl, slot, send_slot, device):
        part = kv_buf.at[slot, :, :, columns(r, cl)]
        return pltpu.make_async_remote_copy(
            src_ref=part, dst_ref=part, send_sem=send_sem.at[cl, send_slot],
            recv_sem=recv_sem.at[r, cl, slot], device_id=device, device_id_type=MESH,
        )

    def events(cl, mode, r):
        first, a_axis = kinds[cl]
        a_next, b_next = (x_next, y_next) if a_axis == "x" else (y_next, x_next)

        def send(slot, send_slot, device):
            copy = copy_of(r, cl, slot, send_slot, device)
            if mode == "end":
                copy.wait_send()
            else:
                @pl.when(r > 0)
                def _():
                    copy.wait_send()

                copy.start()

        def receive(slot):
            if mode == "go":
                copy_of(r, cl, slot, 0, sibling).wait_recv()

        def up(slot, a, cz):
            @pl.when(has_up)
            def _():
                send(slot, a * 5 + cz, z_up)

        def down(slot, a, cz, start=False):
            @pl.when(has_down)
            def _():
                send(slot, a * 5 + (NZ if start else cz), z_down)

        def to_a(slot, cz):
            send(slot, 10 + cz, a_next)

        def to_b(slot, a, cz):
            send(slot, 14 + a * NZ + cz, b_next)

        found = []

        def begin():
            up(own, 0, z)
            down(own, 0, z, True)
            to_a(own, z)
            to_b(own, 0, z)

        found.append((0, begin))

        def along(d, a, upward):
            def event():
                cz = z - d if upward else z + d

                @pl.when(cz >= 0 if upward else cz < NZ)
                def _():
                    slot = place(cl, a, 0, cz)
                    receive(slot)
                    if d < NZ - 1:
                        (up if upward else down)(slot, a, cz)
                    if first == "z":
                        to_a(slot, cz)
                    to_b(slot, a, cz)
            return event

        def from_a(d, sign):
            def event():
                cz = z + sign * d

                def take():
                    slot = place(cl, 1, 0, cz)
                    receive(slot)
                    if first == "a":
                        up(slot, 1, cz)
                        down(slot, 1, cz, True)
                    to_b(slot, 1, cz)

                if d == 0:
                    take()
                else:
                    pl.when(cz >= 0 if sign < 0 else cz < NZ)(take)
            return event

        found.append((1, from_a(0, 1)))
        for d in range(1, NZ):
            for upward in (True, False):
                found.append((d, along(d, 0, upward)))
            if first == "a":
                for upward in (True, False):
                    found.append((d + 1, along(d, 1, upward)))
            else:
                for sign in (-1, 1):
                    found.append((d + 1, from_a(d, sign)))
        return found

    def run_depth(depth, mode, r):
        for cl in (2, 3, 0, 1):
            for at, event in events(cl, mode, r):
                if at == depth:
                    event()

    def leaves(cl, r):
        for a in range(2):
            for cz in range(NZ):
                copy_of(r, cl, place(cl, a, 1, cz), 0, sibling).wait_recv()

    def attend(cl, r):
        cols = columns(r, cl)
        head_keys = kv_buf[:, 0, :, cols].reshape(CHIPS * 2 * rows_each, HD)
        head_values = kv_buf[:, 1, :, cols].reshape(CHIPS * 2 * rows_each, HD)
        widened = jnp.concatenate([head_values, jnp.ones_like(head_values)], axis=1)
        for block in range(2 * q_rows // BLK):
            rows = pl.ds(block * BLK, BLK)
            scores = lax.dot_general(
                q_buf[rows, cols], head_keys, (((1,), (1,)), ((), ())),
                preferred_element_type=jnp.float32,
            )
            per = q_rows // BLK
            scores = scores * FACTOR + bias_buf[block // per, block % per, 0:1, :]
            raised = jnp.exp2(scores - jnp.max(scores, axis=1, keepdims=True)).astype(jnp.bfloat16)
            both = jnp.dot(raised, widened, preferred_element_type=jnp.float32)
            o_buf[rows, cols] = (both[:, :HD] / both[:, HD:]).astype(jnp.bfloat16)

    def out_copies(r):
        cols = pl.ds(pl.multiple_of(r * ROUND_COLS, ROUND_COLS), ROUND_COLS)
        target = out_ref.at[:, pl.ds(pl.multiple_of(core * HALF + r * ROUND_COLS, ROUND_COLS), ROUND_COLS)]
        keep = pltpu.make_async_copy(o_buf.at[q_mine, cols], target, out_sem.at[r])
        give = pltpu.make_async_remote_copy(
            src_ref=o_buf.at[q_theirs, cols], dst_ref=target, send_sem=out_send.at[r],
            recv_sem=out_recv.at[r], device_id=sibling, device_id_type=MESH,
        )
        return keep, give

    def round_body(r, carry):
        @pl.when(r < ROUNDS)
        def _():
            run_depth(0, "go", r)

        @pl.when(r == 0)
        def _():
            for i in (2, 3):
                locals_[i].wait()
                swaps[i].wait_recv()

        for step in range(CLASSES):
            @pl.when(r > 0)
            def _():
                leaves(step, r - 1)
                attend(step, r - 1)

            @pl.when(r < ROUNDS)
            def _():
                run_depth(step + 1, "go", r)

        @pl.when(r > 0)
        def _():
            for copy in out_copies(r - 1):
                copy.start()

        return carry

    lax.fori_loop(0, ROUNDS + 1, round_body, 0)

    for depth in range(NZ + 1):
        run_depth(depth, "end", ROUNDS - 1)
    for copy in swaps:
        copy.wait_send()

    def finish(r, carry):
        keep, give = out_copies(r)
        keep.wait()
        give.wait()
        return carry

    lax.fori_loop(0, ROUNDS, finish, 0)


def gathered(queries, keys, values, key_lists, counts):
    q_rows, rows_each = queries.shape[0], keys.shape[0]
    per = q_rows // BLK
    key_total = CHIPS * 2 * rows_each
    position = np.arange(key_total)
    slot, core = position // (2 * rows_each), position // rows_each % 2
    slot_x, slot_z, slot_y = slot % NX, slot // NX % NZ, slot // (NX * NZ)
    device = (slot_y * 2 + core) * (NZ * NX) + slot_z * NX + slot_x
    block_of = jnp.asarray(device * rows_each // BLK, jnp.int32)
    start = lax.axis_index("kv") * per
    lists = lax.dynamic_slice_in_dim(key_lists, start, per, 0)
    used = lax.dynamic_slice_in_dim(counts, start, per, 0)
    named = jnp.arange(MOST, dtype=jnp.int32)[None, :] < used[:, None]
    hit = jnp.any((lists[:, :, None] == block_of[None, None, :]) & named[:, :, None], axis=1)
    bias = jnp.where(hit, 0.0, -1e30).astype(jnp.float32)
    bias = jnp.broadcast_to(bias[:, None, :], (per, 8, key_total))
    anywhere = pl.BlockSpec(memory_space=pl.ANY)
    flops = 4 * 2 * q_rows * key_total * HALF
    return pl.pallas_call(
        functools.partial(gather_kernel, rows_each, q_rows),
        out_shape=jax.ShapeDtypeStruct(queries.shape, jnp.bfloat16),
        in_specs=[anywhere] * 4,
        out_specs=anywhere,
        scratch_shapes=[
            pltpu.VMEM((CHIPS, 2, 2 * rows_each, HALF), jnp.bfloat16),
            pltpu.VMEM((2 * q_rows, HALF), jnp.bfloat16),
            pltpu.VMEM((2, per, 8, key_total), jnp.float32),
            pltpu.VMEM((2 * q_rows, HALF), jnp.bfloat16),
            pltpu.SemaphoreType.DMA((ROUNDS, CLASSES, CHIPS)),
            pltpu.SemaphoreType.DMA((CLASSES, 22)),
            pltpu.SemaphoreType.DMA((4,)),
            pltpu.SemaphoreType.DMA((4,)),
            pltpu.SemaphoreType.DMA((4,)),
            pltpu.SemaphoreType.DMA((ROUNDS,)),
            pltpu.SemaphoreType.DMA((ROUNDS,)),
            pltpu.SemaphoreType.DMA((ROUNDS,)),
        ],
        compiler_params=pltpu.CompilerParams(
            collective_id=0, has_side_effects=True, vmem_limit_bytes=48 * 1024 * 1024
        ),
        cost_estimate=pl.CostEstimate(flops=flops, bytes_accessed=2 * queries.size * 2, transcendentals=0),
    )(queries, keys, values, bias)


def regroup(split_array, kv_count, pb_count):
    tokens_each = split_array.shape[0] // (kv_count * pb_count)
    shaped = split_array.reshape(kv_count, pb_count, tokens_each, split_array.shape[1])
    return shaped.transpose(1, 0, 2, 3).reshape(-1, split_array.shape[1])


def per_device(queries, keys, values, key_lists, counts):
    kv_count = lax.axis_size("kv")
    pb_count = lax.axis_size("pb")
    head_local = HEADS // kv_count
    scaling = HD ** (-0.5)
    key_whole, value_whole = (
        lax.all_gather(keys, "pb", axis=0, tiled=True),
        lax.all_gather(values, "pb", axis=0, tiled=True),
    )
    key_split, value_split = (
        lax.all_to_all(key_whole, "kv", split_axis=1, concat_axis=0, tiled=True),
        lax.all_to_all(value_whole, "kv", split_axis=1, concat_axis=0, tiled=True),
    )
    key_heads = regroup(key_split, kv_count, pb_count)
    value_heads = regroup(value_split, kv_count, pb_count)
    key_blocks = key_heads.reshape(-1, BLK, head_local, HD)
    value_blocks = value_heads.reshape(-1, BLK, head_local, HD)
    slot_of_key = jnp.arange(MOST * BLK, dtype=jnp.int32) // BLK

    def padded_group(item):
        group_queries, group_lists, group_counts = item
        members = group_queries.shape[0]
        listed_keys = key_blocks[group_lists].reshape(members, MOST * BLK, head_local, HD)
        listed_values = value_blocks[group_lists].reshape(members, MOST * BLK, head_local, HD)
        scores = (
            jnp.einsum(
                "gqhd,gkhd->ghqk", group_queries, listed_keys, preferred_element_type=jnp.float32
            )
            * scaling
        )
        usable = (slot_of_key[None, :] < group_counts[:, None])[:, None, None, :]
        largest = jnp.max(jnp.where(usable, scores, -jnp.inf), axis=-1, keepdims=True)
        raised = jnp.where(usable, jnp.exp(scores - largest), 0.0)
        totals = jnp.sum(raised, axis=-1, keepdims=True)
        weights = (raised / totals).astype(jnp.bfloat16)
        output = jnp.einsum(
            "ghqk,gkhd->gqhd", weights, listed_values, preferred_element_type=jnp.float32
        )
        return output.astype(jnp.bfloat16)

    query_blocks = queries.reshape(-1, BLK, queries.shape[1])
    exchanged = lax.all_to_all(query_blocks, "kv", split_axis=2, concat_axis=0, tiled=True)
    block_total = exchanged.shape[0]
    rows = exchanged.shape[1]
    per_group = math.gcd(block_total, max(1, 512 // rows))
    group_total = block_total // per_group
    grouped = exchanged.reshape(group_total, per_group, rows, head_local, HD)
    lists_grouped = key_lists.reshape(group_total, per_group, key_lists.shape[1])
    counts_grouped = counts.reshape(group_total, per_group)
    produced = lax.map(padded_group, (grouped, lists_grouped, counts_grouped))
    joined = produced.reshape(block_total, rows, head_local * HD)
    result = lax.all_to_all(joined, "kv", split_axis=0, concat_axis=2, tiled=True)
    return result.reshape(queries.shape)


def solution(mesh):
    fits = mesh.shape["pb"] == NY * 2 and mesh.shape["kv"] == NX * NZ

    def choose(queries, keys, values, key_lists, counts):
        small = keys.shape[0] == 32 and queries.shape[0] % BLK == 0
        work = gathered if fits and small else per_device
        return work(queries, keys, values, key_lists, counts)

    return jax.shard_map(
        choose,
        mesh=mesh,
        in_specs=(
            P(("pb", "kv"), None),
            P(("pb", "kv"), None),
            P(("pb", "kv"), None),
            P("pb", None),
            P("pb"),
        ),
        out_specs=P(("pb", "kv"), None),
        check_vma=False,
    )
```

```python
import functools
import math

import jax
import jax.numpy as jnp
from jax import lax
from jax.experimental import pallas as pl
from jax.experimental.pallas import tpu as pltpu
from jax.sharding import PartitionSpec as P

HEADS = 32
HD = 128
BLK = 128
MOST = 8

NX, NY, NZ = 2, 2, 4
CHIPS = NX * NY * NZ
HALF = HEADS // 2 * HD
CLASSES = 4
ROUNDS = HEADS // 2 // CLASSES
ROUND_COLS = CLASSES * HD
MESH = pl.DeviceIdType.MESH
FACTOR = HD ** (-0.5) * math.log2(math.e)


def key_block(slot, core, rows_each):
    cx, cz, cy = slot % NX, slot // NX % NZ, slot // (NX * NZ)
    return ((cy * 2 + core) * (NZ * NX) + cz * NX + cx) * rows_each // BLK


def gather_kernel(
    rows_each, q_rows, q_ref, k_ref, v_ref, bias_ref, out_ref,
    kv_buf, q_buf, bias_buf, extra_buf, o_buf,
    recv_sem, send_sem, load_sem, swap_send, swap_recv, out_sem, out_send, out_recv,
):
    pb, kv = lax.axis_index("pb"), lax.axis_index("kv")
    y, core = pb // 2, pb % 2
    z, x = kv // 2, kv % 2
    other = 1 - core
    sibling = (y * 2 + other, kv)
    x_next = (pb, z * 2 + (1 - x))
    y_next = ((1 - y) * 2 + core, kv)
    z_up = (pb, kv + 2)
    z_down = (pb, kv - 2)
    has_up, has_down = z < NZ - 1, z > 0

    barrier = pltpu.get_barrier_semaphore()

    def greet(device):
        pl.semaphore_signal(barrier, inc=1, device_id=device, device_id_type=MESH)

    greet(sibling)
    greet(x_next)
    greet(y_next)

    @pl.when(has_up)
    def _():
        greet(z_up)

    @pl.when(has_down)
    def _():
        greet(z_down)

    def slot_at(cx, cy, cz):
        return (cy * NZ + cz) * NX + cx

    own = slot_at(x, y, z)
    mine = pl.ds(pl.multiple_of(core * HALF, HALF), HALF)
    theirs = pl.ds(pl.multiple_of(other * HALF, HALF), HALF)
    tokens = pl.ds(pl.multiple_of(core * rows_each, rows_each), rows_each)
    q_mine = pl.ds(pl.multiple_of(core * q_rows, q_rows), q_rows)
    q_theirs = pl.ds(pl.multiple_of(other * q_rows, q_rows), q_rows)
    pairs = [
        (k_ref, kv_buf.at[own, 0, tokens, :]),
        (v_ref, kv_buf.at[own, 1, tokens, :]),
        (q_ref, q_buf.at[q_mine, :]),
    ]
    locals_ = [
        pltpu.make_async_copy(source.at[:, mine], target, load_sem.at[i])
        for i, (source, target) in enumerate(pairs)
    ]
    locals_.append(pltpu.make_async_copy(bias_ref, bias_buf.at[core], load_sem.at[3]))
    for copy in locals_:
        copy.start()

    pl.semaphore_wait(barrier, 3 + has_up.astype(jnp.int32) + has_down.astype(jnp.int32))

    def swap(source, target, i):
        return pltpu.make_async_remote_copy(
            src_ref=source, dst_ref=target, send_sem=swap_send.at[i], recv_sem=swap_recv.at[i],
            device_id=sibling, device_id_type=MESH,
        )

    swaps = [swap(source.at[:, theirs], target, i) for i, (source, target) in enumerate(pairs)]
    swaps.append(swap(bias_ref, bias_buf.at[core], 3))
    for i in (0, 1, 3):
        swaps[i].start()
    for i in range(2):
        locals_[i].wait()
        swaps[i].wait_recv()

    kinds = [("z", "x"), ("z", "y"), ("a", "x"), ("a", "y")]

    def columns(r, cl):
        return pl.ds(pl.multiple_of(r * ROUND_COLS + cl * HD, HD), HD)

    def place(cl, a, b, cz):
        a_axis = kinds[cl][1]
        dx, dy = (a, b) if a_axis == "x" else (b, a)
        return slot_at(1 - x if dx else x, 1 - y if dy else y, cz)

    def copy_of(r, cl, slot, send_slot, device):
        part = kv_buf.at[slot, :, :, columns(r, cl)]
        return pltpu.make_async_remote_copy(
            src_ref=part, dst_ref=part, send_sem=send_sem.at[cl, send_slot],
            recv_sem=recv_sem.at[r, cl, slot], device_id=device, device_id_type=MESH,
        )

    def events(cl, mode, r):
        first, a_axis = kinds[cl]
        a_next, b_next = (x_next, y_next) if a_axis == "x" else (y_next, x_next)

        def send(slot, send_slot, device):
            copy = copy_of(r, cl, slot, send_slot, device)
            if mode == "end":
                copy.wait_send()
            else:
                @pl.when(r > 0)
                def _():
                    copy.wait_send()

                copy.start()

        def receive(slot):
            if mode == "go":
                copy_of(r, cl, slot, 0, sibling).wait_recv()

        def up(slot, a, cz):
            @pl.when(has_up)
            def _():
                send(slot, a * 5 + cz, z_up)

        def down(slot, a, cz, start=False):
            @pl.when(has_down)
            def _():
                send(slot, a * 5 + (NZ if start else cz), z_down)

        def to_a(slot, cz):
            send(slot, 10 + cz, a_next)

        def to_b(slot, a, cz):
            send(slot, 14 + a * NZ + cz, b_next)

        found = []

        def begin():
            up(own, 0, z)
            down(own, 0, z, True)
            to_a(own, z)
            to_b(own, 0, z)

        found.append((0, begin))

        def along(d, a, upward):
            def event():
                cz = z - d if upward else z + d

                @pl.when(cz >= 0 if upward else cz < NZ)
                def _():
                    slot = place(cl, a, 0, cz)
                    receive(slot)
                    if d < NZ - 1:
                        (up if upward else down)(slot, a, cz)
                    if first == "z":
                        to_a(slot, cz)
                    to_b(slot, a, cz)
            return event

        def from_a(d, sign):
            def event():
                cz = z + sign * d

                def take():
                    slot = place(cl, 1, 0, cz)
                    receive(slot)
                    if first == "a":
                        up(slot, 1, cz)
                        down(slot, 1, cz, True)
                    to_b(slot, 1, cz)

                if d == 0:
                    take()
                else:
                    pl.when(cz >= 0 if sign < 0 else cz < NZ)(take)
            return event

        found.append((1, from_a(0, 1)))
        for d in range(1, NZ):
            for upward in (True, False):
                found.append((d, along(d, 0, upward)))
            if first == "a":
                for upward in (True, False):
                    found.append((d + 1, along(d, 1, upward)))
            else:
                for sign in (-1, 1):
                    found.append((d + 1, from_a(d, sign)))
        return found

    order = [(depth, cl) for depth in range(NZ + 1) for cl in (2, 3, 0, 1)]

    def run_group(index, mode, r):
        depth, cl = order[index]
        for at, event in events(cl, mode, r):
            if at == depth:
                event()

    def begin_round(r):
        for index in range(CLASSES):
            run_group(index, "go", r)

    def leaves(cl, r):
        for a in range(2):
            for cz in range(NZ):
                copy_of(r, cl, place(cl, a, 1, cz), 0, sibling).wait_recv()

    def attend(cl, r, blocks):
        cols = columns(r, cl)
        total = CHIPS * 2 * rows_each
        head_keys = jnp.concatenate([kv_buf[:, 0, :, cols].reshape(total, HD), extra_buf[...]], axis=1)
        head_values = kv_buf[:, 1, :, cols].reshape(total, HD)
        head_values = jnp.concatenate([head_values, jnp.ones_like(head_values)], axis=1)
        lane = lax.broadcasted_iota(jnp.int32, (BLK, HD), 1)
        scores = []
        for block in blocks:
            chosen = jnp.where(lane == block, 1.0, 0.0).astype(jnp.bfloat16)
            head_queries = jnp.concatenate([q_buf[pl.ds(block * BLK, BLK), cols], chosen], axis=1)
            scores.append(lax.dot_general(
                head_queries, head_keys, (((1,), (1,)), ((), ())), preferred_element_type=jnp.float32
            ))
        for block, found in zip(blocks, scores):
            largest = jnp.max(found, axis=1, keepdims=True)
            raised = jnp.exp2((found - largest) * FACTOR).astype(jnp.bfloat16)
            both = jnp.dot(raised, head_values, preferred_element_type=jnp.float32)
            o_buf[pl.ds(block * BLK, BLK), cols] = (both[:, :HD] / both[:, HD:]).astype(jnp.bfloat16)

    def out_copies(r):
        cols = pl.ds(pl.multiple_of(r * ROUND_COLS, ROUND_COLS), ROUND_COLS)
        target = out_ref.at[:, pl.ds(pl.multiple_of(core * HALF + r * ROUND_COLS, ROUND_COLS), ROUND_COLS)]
        keep = pltpu.make_async_copy(o_buf.at[q_mine, cols], target, out_sem.at[r])
        give = pltpu.make_async_remote_copy(
            src_ref=o_buf.at[q_theirs, cols], dst_ref=target, send_sem=out_send.at[r],
            recv_sem=out_recv.at[r], device_id=sibling, device_id_type=MESH,
        )
        return keep, give

    blocks_each = 2 * q_rows // BLK // 2

    def round_body(r, carry):
        @pl.when(r < ROUNDS)
        def _():
            for index in range(CLASSES, 2 * CLASSES):
                run_group(index, "go", r)

        for step in range(2 * CLASSES):
            cl, part = step // 2, step % 2

            @pl.when(r > 0)
            def _():
                if part == 0:
                    leaves(cl, r - 1)
                attend(cl, r - 1, range(part * blocks_each, (part + 1) * blocks_each))

            @pl.when(r < ROUNDS)
            def _():
                for index in range(2 * CLASSES + step * 3 // 2, 2 * CLASSES + (step + 1) * 3 // 2):
                    run_group(index, "go", r)

            if step == CLASSES:
                @pl.when(r < ROUNDS - 1)
                def _():
                    begin_round(r + 1)

        @pl.when(r > 0)
        def _():
            for copy in out_copies(r - 1):
                copy.start()

        return carry

    begin_round(0)
    swaps[2].start()
    for i in (2, 3):
        locals_[i].wait()
        swaps[i].wait_recv()
    marks = bias_buf[0] + bias_buf[1]
    for slot in range(CHIPS):
        for side in range(2):
            block = key_block(slot, side, rows_each)
            start = (slot * 2 + side) * rows_each
            extra_buf[pl.ds(start, rows_each), :] = jnp.broadcast_to(
                marks[block:block + 1, :], (rows_each, HD)
            ).astype(jnp.bfloat16)

    lax.fori_loop(0, ROUNDS + 1, round_body, 0)

    for index in range(len(order)):
        run_group(index, "end", ROUNDS - 1)
    for copy in swaps:
        copy.wait_send()

    def finish(r, carry):
        keep, give = out_copies(r)
        keep.wait()
        give.wait()
        return carry

    lax.fori_loop(0, ROUNDS, finish, 0)


def gathered(queries, keys, values, key_lists, counts):
    q_rows, rows_each = queries.shape[0], keys.shape[0]
    per = q_rows // BLK
    key_total = CHIPS * 2 * rows_each
    first = lax.axis_index("pb") % 2 * per
    lane = jnp.arange(HD, dtype=jnp.int32)
    row_of_lane = lax.axis_index("kv") * per + lane - first
    valid = (lane >= first) & (lane < first + per)
    block = jnp.arange(key_total // BLK, dtype=jnp.int32)[:, None, None, None]
    same_row = jnp.arange(key_lists.shape[0], dtype=jnp.int32)[None, None, :, None] == row_of_lane[None, :, None, None]
    named = jnp.arange(MOST, dtype=jnp.int32)[None, :] < counts[:, None]
    hit = jnp.any((key_lists[None, None] == block) & named[None, None] & same_row, axis=(2, 3))
    bias = jnp.where(valid[None, :] & ~hit, -1e30, 0.0).astype(jnp.float32)
    anywhere = pl.BlockSpec(memory_space=pl.ANY)
    flops = 4 * 2 * q_rows * key_total * HALF
    return pl.pallas_call(
        functools.partial(gather_kernel, rows_each, q_rows),
        out_shape=jax.ShapeDtypeStruct(queries.shape, jnp.bfloat16),
        in_specs=[anywhere] * 4,
        out_specs=anywhere,
        scratch_shapes=[
            pltpu.VMEM((CHIPS, 2, 2 * rows_each, HALF), jnp.bfloat16),
            pltpu.VMEM((2 * q_rows, HALF), jnp.bfloat16),
            pltpu.VMEM((2, key_total // BLK, HD), jnp.float32),
            pltpu.VMEM((key_total, HD), jnp.bfloat16),
            pltpu.VMEM((2 * q_rows, HALF), jnp.bfloat16),
            pltpu.SemaphoreType.DMA((ROUNDS, CLASSES, CHIPS)),
            pltpu.SemaphoreType.DMA((CLASSES, 22)),
            pltpu.SemaphoreType.DMA((4,)),
            pltpu.SemaphoreType.DMA((4,)),
            pltpu.SemaphoreType.DMA((4,)),
            pltpu.SemaphoreType.DMA((ROUNDS,)),
            pltpu.SemaphoreType.DMA((ROUNDS,)),
            pltpu.SemaphoreType.DMA((ROUNDS,)),
        ],
        compiler_params=pltpu.CompilerParams(
            collective_id=0, has_side_effects=True, vmem_limit_bytes=61 * 1024 * 1024
        ),
        cost_estimate=pl.CostEstimate(flops=flops, bytes_accessed=2 * queries.size * 2, transcendentals=0),
    )(queries, keys, values, bias)


def regroup(split_array, kv_count, pb_count):
    tokens_each = split_array.shape[0] // (kv_count * pb_count)
    shaped = split_array.reshape(kv_count, pb_count, tokens_each, split_array.shape[1])
    return shaped.transpose(1, 0, 2, 3).reshape(-1, split_array.shape[1])


def per_device(queries, keys, values, key_lists, counts):
    kv_count = lax.axis_size("kv")
    pb_count = lax.axis_size("pb")
    head_local = HEADS // kv_count
    scaling = HD ** (-0.5)
    key_whole, value_whole = (
        lax.all_gather(keys, "pb", axis=0, tiled=True),
        lax.all_gather(values, "pb", axis=0, tiled=True),
    )
    key_split, value_split = (
        lax.all_to_all(key_whole, "kv", split_axis=1, concat_axis=0, tiled=True),
        lax.all_to_all(value_whole, "kv", split_axis=1, concat_axis=0, tiled=True),
    )
    key_heads = regroup(key_split, kv_count, pb_count)
    value_heads = regroup(value_split, kv_count, pb_count)
    key_blocks = key_heads.reshape(-1, BLK, head_local, HD)
    value_blocks = value_heads.reshape(-1, BLK, head_local, HD)
    slot_of_key = jnp.arange(MOST * BLK, dtype=jnp.int32) // BLK

    def padded_group(item):
        group_queries, group_lists, group_counts = item
        members = group_queries.shape[0]
        listed_keys = key_blocks[group_lists].reshape(members, MOST * BLK, head_local, HD)
        listed_values = value_blocks[group_lists].reshape(members, MOST * BLK, head_local, HD)
        scores = (
            jnp.einsum(
                "gqhd,gkhd->ghqk", group_queries, listed_keys, preferred_element_type=jnp.float32
            )
            * scaling
        )
        usable = (slot_of_key[None, :] < group_counts[:, None])[:, None, None, :]
        largest = jnp.max(jnp.where(usable, scores, -jnp.inf), axis=-1, keepdims=True)
        raised = jnp.where(usable, jnp.exp(scores - largest), 0.0)
        totals = jnp.sum(raised, axis=-1, keepdims=True)
        weights = (raised / totals).astype(jnp.bfloat16)
        output = jnp.einsum(
            "ghqk,gkhd->gqhd", weights, listed_values, preferred_element_type=jnp.float32
        )
        return output.astype(jnp.bfloat16)

    query_blocks = queries.reshape(-1, BLK, queries.shape[1])
    exchanged = lax.all_to_all(query_blocks, "kv", split_axis=2, concat_axis=0, tiled=True)
    block_total = exchanged.shape[0]
    rows = exchanged.shape[1]
    per_group = math.gcd(block_total, max(1, 512 // rows))
    group_total = block_total // per_group
    grouped = exchanged.reshape(group_total, per_group, rows, head_local, HD)
    lists_grouped = key_lists.reshape(group_total, per_group, key_lists.shape[1])
    counts_grouped = counts.reshape(group_total, per_group)
    produced = lax.map(padded_group, (grouped, lists_grouped, counts_grouped))
    joined = produced.reshape(block_total, rows, head_local * HD)
    result = lax.all_to_all(joined, "kv", split_axis=0, concat_axis=2, tiled=True)
    return result.reshape(queries.shape)


def solution(mesh):
    fits = mesh.shape["pb"] == NY * 2 and mesh.shape["kv"] == NX * NZ

    def choose(queries, keys, values, key_lists, counts):
        small = keys.shape[0] == 32 and queries.shape[0] % BLK == 0
        work = gathered if fits and small else per_device
        return work(queries, keys, values, key_lists, counts)

    return jax.shard_map(
        choose,
        mesh=mesh,
        in_specs=(
            P(("pb", "kv"), None),
            P(("pb", "kv"), None),
            P(("pb", "kv"), None),
            P("pb", None),
            P("pb"),
        ),
        out_specs=P(("pb", "kv"), None),
        check_vma=False,
    )
```

```python
import functools
import math

import jax
import jax.numpy as jnp
from jax import lax
from jax.experimental import pallas as pl
from jax.experimental.pallas import tpu as pltpu
from jax.sharding import PartitionSpec as P

HEADS = 32
HD = 128
BLK = 128
MOST = 8

NX, NY, NZ = 2, 2, 4
CHIPS = NX * NY * NZ
HALF = HEADS // 2 * HD
SERVED = HALF // 4
ROUNDS = SERVED // HD
MESH = pl.DeviceIdType.MESH
FACTOR = HD ** (-0.5) * math.log2(math.e)


def axis_coords(axis, a, b, cz):
    return (a, b, cz) if axis == 0 else (b, a, cz)


def key_block(axis, slot, quarter, rows_each):
    cx, cy, cz = axis_coords(axis, quarter // 2, slot // NZ, slot % NZ)
    return ((cy * 2 + quarter % 2) * (NZ * NX) + cz * NX + cx) * rows_each // BLK


def gather_kernel(
    rows_each, q_rows, q_ref, k_ref, v_ref, bias_ref, out_ref,
    kv_buf, q_buf, bias_buf, extra_buf, o_buf,
    recv_sem, send_sem, load_sem, swap_send, swap_recv, out_sem, out_send, out_recv,
):
    pb, kv = lax.axis_index("pb"), lax.axis_index("kv")
    y, core = pb // 2, pb % 2
    z, x = kv // 2, kv % 2
    coord = (x, y)

    def device(axis, flip, swap):
        cx = 1 - x if flip and axis == 0 else x
        cy = 1 - y if flip and axis == 1 else y
        return (cy * 2 + (1 - core if swap else core), z * 2 + cx)

    peers = ((0, 1), (1, 0), (1, 1))
    z_up = (pb, kv + 2)
    z_down = (pb, kv - 2)
    has_up, has_down = z < NZ - 1, z > 0

    barrier = pltpu.get_barrier_semaphore()

    def greet(target):
        pl.semaphore_signal(barrier, inc=1, device_id=target, device_id_type=MESH)

    greet(device(0, 0, 1))
    for axis in range(2):
        greet(device(axis, 1, 0))
        greet(device(axis, 1, 1))

    @pl.when(has_up)
    def _():
        greet(z_up)

    @pl.when(has_down)
    def _():
        greet(z_down)

    def heads_of(axis, flip, swap):
        c = 1 - core if swap else core
        a = 1 - coord[axis] if flip else coord[axis]
        return pl.ds(pl.multiple_of(c * HALF + axis * (HALF // 2) + a * SERVED, SERVED), SERVED)

    def quarter(axis):
        return coord[axis] * 2 + core

    def own(axis):
        return coord[1 - axis] * NZ + z

    def parts(axis, flip, swap):
        cols = heads_of(axis, flip, swap)
        mine = quarter(axis)
        tokens = pl.ds(pl.multiple_of(mine * rows_each, rows_each), rows_each)
        return [
            (k_ref.at[:, cols], kv_buf.at[axis, own(axis), 0, tokens, :]),
            (v_ref.at[:, cols], kv_buf.at[axis, own(axis), 1, tokens, :]),
            (bias_ref.at[axis], bias_buf.at[axis, mine]),
            (q_ref.at[:, cols], q_buf.at[axis, mine]),
        ]

    def load(axis, i):
        source, target = parts(axis, 0, 0)[i]
        return pltpu.make_async_copy(source, target, load_sem.at[axis, i])

    def swap_copy(axis, p, i):
        source, target = parts(axis, *peers[p])[i]
        return pltpu.make_async_remote_copy(
            src_ref=source, dst_ref=target, send_sem=swap_send.at[axis, p, i], recv_sem=swap_recv.at[axis, p, i],
            device_id=device(axis, *peers[p]), device_id_type=MESH,
        )

    for i in range(4):
        for axis in range(2):
            load(axis, i).start()

    pl.semaphore_wait(barrier, 5 + has_up.astype(jnp.int32) + has_down.astype(jnp.int32))

    def start_swaps(kinds):
        for p in range(3):
            for i in kinds:
                for axis in range(2):
                    swap_copy(axis, p, i).start()

    def wait_swaps(kinds):
        for i in kinds:
            for axis in range(2):
                load(axis, i).wait()
                for p in range(3):
                    swap_copy(axis, p, i).wait_recv()

    def copy_of(r, axis, slot, send_slot, target):
        cols = pl.ds(pl.multiple_of(r * HD, HD), HD)
        part = kv_buf.at[axis, slot, :, :, cols]
        return pltpu.make_async_remote_copy(
            src_ref=part, dst_ref=part, send_sem=send_sem.at[r, axis, send_slot],
            recv_sem=recv_sem.at[r, axis, slot], device_id=target, device_id_type=MESH,
        )

    def place(axis, b, cz):
        return (1 - coord[1 - axis] if b else coord[1 - axis]) * NZ + cz

    class Steps:
        def __init__(self, r, axis, across_first, ending):
            self.r, self.axis, self.across_first, self.ending = r, axis, across_first, ending

        def send(self, slot, send_slot, target):
            copy = copy_of(self.r, self.axis, slot, send_slot, target)
            if self.ending:
                copy.wait_send()
            else:
                copy.start()

        def receive(self, slot):
            if not self.ending:
                copy_of(self.r, self.axis, slot, 0, z_up).wait_recv()

        def up(self, b, cz):
            @pl.when(has_up)
            def _():
                self.send(place(self.axis, b, cz), b * 5 + cz, z_up)

        def down(self, b, cz, start=False):
            @pl.when(has_down)
            def _():
                self.send(place(self.axis, b, cz), b * 5 + (NZ if start else cz), z_down)

        def across(self, cz):
            self.send(place(self.axis, 0, cz), 10 + cz, device(1 - self.axis, 1, 0))

        def begin(self):
            if self.across_first:
                self.across(z)
            self.up(0, z)
            self.down(0, z, True)
            if not self.across_first:
                self.across(z)

        def crossed(self):
            self.receive(place(self.axis, 1, z))
            self.up(1, z)
            self.down(1, z, True)

        def along(self, d, b):
            for upward in (True, False):
                cz = z - d if upward else z + d

                @pl.when(cz >= 0 if upward else cz < NZ)
                def _():
                    self.receive(place(self.axis, b, cz))
                    if d < NZ - 1:
                        (self.up if upward else self.down)(b, cz)
                    if not self.across_first:
                        self.across(cz)

    def first_round(ending):
        steps = [Steps(0, axis, True, ending) for axis in range(2)]
        if ending:
            for step in steps:
                step.begin()
        for step in steps:
            step.crossed()
        for d in range(1, NZ):
            for b in range(2):
                for step in steps:
                    step.along(d, b)

    def begin_round(r):
        for axis in range(2):
            Steps(r, axis, False, False).begin()

    def later_group(index, r):
        Steps(r, index % 2, False, False).along(1 + index // 2, 0)

    def leaves(axis, r):
        for cz in range(NZ):
            copy_of(r, axis, place(axis, 1, cz), 0, z_up).wait_recv()

    def attend(axis, r, pair):
        cols = pl.ds(pl.multiple_of(r * HD, HD), HD)
        total = 2 * NZ * 4 * rows_each
        head_keys = jnp.concatenate([kv_buf[axis, :, 0, :, cols].reshape(total, HD), extra_buf[axis]], axis=1)
        head_values = kv_buf[axis, :, 1, :, cols].reshape(total, HD)
        head_values = jnp.concatenate([head_values, jnp.ones_like(head_values)], axis=1)
        lane = lax.broadcasted_iota(jnp.int32, (BLK, HD), 1)
        per = q_rows // BLK
        scores = []
        for block in range(per):
            chosen = jnp.where(lane == pair * per + block, 1.0, 0.0).astype(jnp.bfloat16)
            head_queries = jnp.concatenate([q_buf[axis, pair, pl.ds(block * BLK, BLK), cols], chosen], axis=1)
            scores.append(lax.dot_general(
                head_queries, head_keys, (((1,), (1,)), ((), ())), preferred_element_type=jnp.float32
            ))
        for block, found in enumerate(scores):
            largest = jnp.max(found, axis=1, keepdims=True)
            raised = jnp.exp2((found - largest) * FACTOR).astype(jnp.bfloat16)
            both = jnp.dot(raised, head_values, preferred_element_type=jnp.float32)
            o_buf[axis, pair, pl.ds(block * BLK, BLK), cols] = (both[:, :HD] / both[:, HD:]).astype(jnp.bfloat16)

    def out_columns(axis, r):
        start = core * HALF + axis * (HALF // 2) + coord[axis] * SERVED + r * HD
        return out_ref.at[:, pl.ds(pl.multiple_of(start, HD), HD)]

    def out_copies(axis, r):
        cols = pl.ds(pl.multiple_of(r * HD, HD), HD)
        found = []
        for p, (flip, swap) in enumerate(peers):
            a = 1 - coord[axis] if flip else coord[axis]
            c = 1 - core if swap else core
            found.append(pltpu.make_async_remote_copy(
                src_ref=o_buf.at[axis, a * 2 + c, :, cols], dst_ref=out_columns(axis, r),
                send_sem=out_send.at[r, axis, p], recv_sem=out_recv.at[r, axis, p],
                device_id=device(axis, flip, swap), device_id_type=MESH,
            ))
        return found

    def out_keep(axis, r):
        cols = pl.ds(pl.multiple_of(r * HD, HD), HD)
        return pltpu.make_async_copy(
            o_buf.at[axis, quarter(axis), :, cols], out_columns(axis, r), out_sem.at[r, axis]
        )

    def round_body(r, carry):
        @pl.when(r < ROUNDS)
        def _():
            later_group(0, r)
            later_group(1, r)

        for step in range(8):
            axis, pair = step // 4, step % 4

            if pair == 0:
                @pl.when(r > 1)
                def _():
                    leaves(axis, r - 1)

            attend(axis, r - 1, pair)
            if pair == 3:
                for copy in reversed(out_copies(axis, r - 1)):
                    copy.start()
                out_keep(axis, r - 1).start()

            if step < 4:
                @pl.when(r < ROUNDS)
                def _():
                    later_group(2 + step, r)

            if step == 4:
                @pl.when(r < ROUNDS - 1)
                def _():
                    begin_round(r + 1)

        return carry

    start_swaps((0, 1, 2))
    wait_swaps((0, 1))
    for axis in range(2):
        Steps(0, axis, True, False).begin()
    start_swaps((3,))
    first_round(False)
    begin_round(1)
    wait_swaps((2, 3))
    for axis in range(2):
        marks = bias_buf[axis, 0] + bias_buf[axis, 1] + bias_buf[axis, 2] + bias_buf[axis, 3]
        for slot in range(2 * NZ):
            for part in range(4):
                block = key_block(axis, slot, part, rows_each)
                start = (slot * 4 + part) * rows_each
                extra_buf[axis, pl.ds(start, rows_each), :] = jnp.broadcast_to(
                    marks[block:block + 1, :], (rows_each, HD)
                ).astype(jnp.bfloat16)

    lax.fori_loop(1, ROUNDS + 1, round_body, 0)

    first_round(True)

    def end_round(r, carry):
        for axis in range(2):
            step = Steps(r, axis, False, True)
            step.begin()
            for d in range(1, NZ):
                step.along(d, 0)
        return carry

    lax.fori_loop(1, ROUNDS, end_round, 0)
    for axis in range(2):
        for p in range(3):
            for i in range(4):
                swap_copy(axis, p, i).wait_send()

    def finish(r, carry):
        for axis in range(2):
            out_keep(axis, r).wait()
            for copy in out_copies(axis, r):
                copy.wait()
        return carry

    lax.fori_loop(0, ROUNDS, finish, 0)


def gathered(queries, keys, values, key_lists, counts):
    q_rows, rows_each = queries.shape[0], keys.shape[0]
    per = q_rows // BLK
    key_total = CHIPS * 2 * rows_each
    pb, kv = lax.axis_index("pb"), lax.axis_index("kv")
    first = (jnp.stack([kv % 2, pb // 2]) * 2 + pb % 2)[:, None] * per
    lane = jnp.arange(HD, dtype=jnp.int32)[None, :]
    row_of_lane = (kv * per + lane - first)[:, None, :, None, None]
    valid = (lane >= first) & (lane < first + per)
    block = jnp.arange(key_total // BLK, dtype=jnp.int32)[None, :, None, None, None]
    same_row = jnp.arange(key_lists.shape[0], dtype=jnp.int32)[None, None, None, :, None] == row_of_lane
    named = jnp.arange(MOST, dtype=jnp.int32)[None, :] < counts[:, None]
    hit = jnp.any((key_lists[None, None, None] == block) & named[None, None, None] & same_row, axis=(3, 4))
    bias = jnp.where(valid[:, None, :] & ~hit, -1e30, 0.0).astype(jnp.float32)
    anywhere = pl.BlockSpec(memory_space=pl.ANY)
    flops = 4 * 2 * q_rows * key_total * HALF
    return pl.pallas_call(
        functools.partial(gather_kernel, rows_each, q_rows),
        out_shape=jax.ShapeDtypeStruct(queries.shape, jnp.bfloat16),
        in_specs=[anywhere] * 4,
        out_specs=pl.BlockSpec(memory_space=pltpu.VMEM),
        scratch_shapes=[
            pltpu.VMEM((2, 2 * NZ, 2, 4 * rows_each, SERVED), jnp.bfloat16),
            pltpu.VMEM((2, 4, q_rows, SERVED), jnp.bfloat16),
            pltpu.VMEM((2, 4, key_total // BLK, HD), jnp.float32),
            pltpu.VMEM((2, key_total, HD), jnp.bfloat16),
            pltpu.VMEM((2, 4, q_rows, SERVED), jnp.bfloat16),
            pltpu.SemaphoreType.DMA((ROUNDS, 2, 2 * NZ)),
            pltpu.SemaphoreType.DMA((ROUNDS, 2, 14)),
            pltpu.SemaphoreType.DMA((2, 4)),
            pltpu.SemaphoreType.DMA((2, 3, 4)),
            pltpu.SemaphoreType.DMA((2, 3, 4)),
            pltpu.SemaphoreType.DMA((ROUNDS, 2)),
            pltpu.SemaphoreType.DMA((ROUNDS, 2, 3)),
            pltpu.SemaphoreType.DMA((ROUNDS, 2, 3)),
        ],
        compiler_params=pltpu.CompilerParams(
            collective_id=0, has_side_effects=True, vmem_limit_bytes=61 * 1024 * 1024
        ),
        cost_estimate=pl.CostEstimate(flops=flops, bytes_accessed=2 * queries.size * 2, transcendentals=0),
    )(queries, keys, values, bias)


def regroup(split_array, kv_count, pb_count):
    tokens_each = split_array.shape[0] // (kv_count * pb_count)
    shaped = split_array.reshape(kv_count, pb_count, tokens_each, split_array.shape[1])
    return shaped.transpose(1, 0, 2, 3).reshape(-1, split_array.shape[1])


def per_device(queries, keys, values, key_lists, counts):
    kv_count = lax.axis_size("kv")
    pb_count = lax.axis_size("pb")
    head_local = HEADS // kv_count
    scaling = HD ** (-0.5)
    key_whole, value_whole = (
        lax.all_gather(keys, "pb", axis=0, tiled=True),
        lax.all_gather(values, "pb", axis=0, tiled=True),
    )
    key_split, value_split = (
        lax.all_to_all(key_whole, "kv", split_axis=1, concat_axis=0, tiled=True),
        lax.all_to_all(value_whole, "kv", split_axis=1, concat_axis=0, tiled=True),
    )
    key_heads = regroup(key_split, kv_count, pb_count)
    value_heads = regroup(value_split, kv_count, pb_count)
    key_blocks = key_heads.reshape(-1, BLK, head_local, HD)
    value_blocks = value_heads.reshape(-1, BLK, head_local, HD)
    slot_of_key = jnp.arange(MOST * BLK, dtype=jnp.int32) // BLK

    def padded_group(item):
        group_queries, group_lists, group_counts = item
        members = group_queries.shape[0]
        listed_keys = key_blocks[group_lists].reshape(members, MOST * BLK, head_local, HD)
        listed_values = value_blocks[group_lists].reshape(members, MOST * BLK, head_local, HD)
        scores = (
            jnp.einsum(
                "gqhd,gkhd->ghqk", group_queries, listed_keys, preferred_element_type=jnp.float32
            )
            * scaling
        )
        usable = (slot_of_key[None, :] < group_counts[:, None])[:, None, None, :]
        largest = jnp.max(jnp.where(usable, scores, -jnp.inf), axis=-1, keepdims=True)
        raised = jnp.where(usable, jnp.exp(scores - largest), 0.0)
        totals = jnp.sum(raised, axis=-1, keepdims=True)
        weights = (raised / totals).astype(jnp.bfloat16)
        output = jnp.einsum(
            "ghqk,gkhd->gqhd", weights, listed_values, preferred_element_type=jnp.float32
        )
        return output.astype(jnp.bfloat16)

    query_blocks = queries.reshape(-1, BLK, queries.shape[1])
    exchanged = lax.all_to_all(query_blocks, "kv", split_axis=2, concat_axis=0, tiled=True)
    block_total = exchanged.shape[0]
    rows = exchanged.shape[1]
    per_group = math.gcd(block_total, max(1, 512 // rows))
    group_total = block_total // per_group
    grouped = exchanged.reshape(group_total, per_group, rows, head_local, HD)
    lists_grouped = key_lists.reshape(group_total, per_group, key_lists.shape[1])
    counts_grouped = counts.reshape(group_total, per_group)
    produced = lax.map(padded_group, (grouped, lists_grouped, counts_grouped))
    joined = produced.reshape(block_total, rows, head_local * HD)
    result = lax.all_to_all(joined, "kv", split_axis=0, concat_axis=2, tiled=True)
    return result.reshape(queries.shape)


def solution(mesh):
    fits = mesh.shape["pb"] == NY * 2 and mesh.shape["kv"] == NX * NZ

    def choose(queries, keys, values, key_lists, counts):
        small = keys.shape[0] == 32 and queries.shape[0] % BLK == 0
        work = gathered if fits and small else per_device
        return work(queries, keys, values, key_lists, counts)

    return jax.shard_map(
        choose,
        mesh=mesh,
        in_specs=(
            P(("pb", "kv"), None),
            P(("pb", "kv"), None),
            P(("pb", "kv"), None),
            P("pb", None),
            P("pb"),
        ),
        out_specs=P(("pb", "kv"), None),
        check_vma=False,
    )
```

```python
import functools
import math

import jax
import jax.numpy as jnp
from jax import lax
from jax.experimental import pallas as pl
from jax.experimental.pallas import tpu as pltpu
from jax.sharding import PartitionSpec as P

HEADS = 32
HD = 128
BLK = 128
MOST = 8

NX, NY, NZ = 2, 2, 4
CHIPS = NX * NY * NZ
HALF = HEADS // 2 * HD
SERVED = HALF // 4
ROUNDS = SERVED // HD
MESH = pl.DeviceIdType.MESH
FACTOR = HD ** (-0.5) * math.log2(math.e)


def axis_coords(axis, a, b, cz):
    return (a, b, cz) if axis == 0 else (b, a, cz)


def key_block(axis, slot, quarter, rows_each):
    cx, cy, cz = axis_coords(axis, quarter // 2, slot // NZ, slot % NZ)
    return ((cy * 2 + quarter % 2) * (NZ * NX) + cz * NX + cx) * rows_each // BLK


def gather_kernel(
    rows_each, q_rows, q_ref, k_ref, v_ref, lists_ref, counts_ref, out_ref,
    kv_buf, q_buf, bias_buf, extra_buf, o_buf,
    recv_sem, send_sem, load_sem, swap_send, swap_recv, out_sem, out_send, out_recv,
):
    pb, kv = lax.axis_index("pb"), lax.axis_index("kv")
    y, core = pb // 2, pb % 2
    z, x = kv // 2, kv % 2
    coord = (x, y)

    def device(axis, flip, swap):
        cx = 1 - x if flip and axis == 0 else x
        cy = 1 - y if flip and axis == 1 else y
        return (cy * 2 + (1 - core if swap else core), z * 2 + cx)

    peers = ((0, 1), (1, 0), (1, 1))
    z_up = (pb, kv + 2)
    z_down = (pb, kv - 2)
    has_up, has_down = z < NZ - 1, z > 0

    barrier = pltpu.get_barrier_semaphore()

    def greet(target):
        pl.semaphore_signal(barrier, inc=1, device_id=target, device_id_type=MESH)

    greet(device(0, 0, 1))
    for axis in range(2):
        greet(device(axis, 1, 0))
        greet(device(axis, 1, 1))

    @pl.when(has_up)
    def _():
        greet(z_up)

    @pl.when(has_down)
    def _():
        greet(z_down)

    def heads_of(axis, flip, swap):
        c = 1 - core if swap else core
        a = 1 - coord[axis] if flip else coord[axis]
        return pl.ds(pl.multiple_of(c * HALF + axis * (HALF // 2) + a * SERVED, SERVED), SERVED)

    def quarter(axis):
        return coord[axis] * 2 + core

    def own(axis):
        return coord[1 - axis] * NZ + z

    def parts(axis, flip, swap):
        cols = heads_of(axis, flip, swap)
        mine = quarter(axis)
        tokens = pl.ds(pl.multiple_of(mine * rows_each, rows_each), rows_each)
        return [
            (k_ref.at[:, cols], kv_buf.at[axis, own(axis), 0, tokens, :]),
            (v_ref.at[:, cols], kv_buf.at[axis, own(axis), 1, tokens, :]),
            (bias_buf.at[axis, mine], bias_buf.at[axis, mine]),
            (q_ref.at[:, cols], q_buf.at[axis, mine]),
        ]

    def load(axis, i):
        source, target = parts(axis, 0, 0)[i]
        return pltpu.make_async_copy(source, target, load_sem.at[axis, i])

    def swap_copy(axis, p, i):
        source, target = parts(axis, *peers[p])[i]
        return pltpu.make_async_remote_copy(
            src_ref=source, dst_ref=target, send_sem=swap_send.at[axis, p, i], recv_sem=swap_recv.at[axis, p, i],
            device_id=device(axis, *peers[p]), device_id_type=MESH,
        )

    for i in (0, 1, 3):
        for axis in range(2):
            load(axis, i).start()

    per = q_rows // BLK
    for axis in range(2):
        tile = bias_buf.shape[2:]
        block_id = lax.broadcasted_iota(jnp.int32, tile, 0)
        lane_id = lax.broadcasted_iota(jnp.int32, tile, 1)
        tally = jnp.zeros(tile, jnp.float32)
        for one in range(per):
            row = kv * per + one
            used = counts_ref[row]
            hit = jnp.zeros(tile, jnp.float32)
            for entry in range(MOST):
                named = jnp.where(entry < used, lists_ref[row, entry], -1)
                hit = jnp.where(block_id == named, 1.0, hit)
            wanted = lane_id == quarter(axis) * per + one
            tally = jnp.where(wanted, jnp.where(hit > 0.5, 0.0, -1e30), tally)
        bias_buf[axis, quarter(axis)] = tally

    pl.semaphore_wait(barrier, 5 + has_up.astype(jnp.int32) + has_down.astype(jnp.int32))

    def start_swaps(kinds):
        for p in range(3):
            for i in kinds:
                for axis in range(2):
                    swap_copy(axis, p, i).start()

    def wait_swaps(kinds):
        for i in kinds:
            for axis in range(2):
                if i != 2:
                    load(axis, i).wait()
                for p in range(3):
                    swap_copy(axis, p, i).wait_recv()

    def copy_of(r, axis, slot, send_slot, target):
        cols = pl.ds(pl.multiple_of(r * HD, HD), HD)
        part = kv_buf.at[axis, slot, :, :, cols]
        return pltpu.make_async_remote_copy(
            src_ref=part, dst_ref=part, send_sem=send_sem.at[r, axis, send_slot],
            recv_sem=recv_sem.at[r, axis, slot], device_id=target, device_id_type=MESH,
        )

    def place(axis, b, cz):
        return (1 - coord[1 - axis] if b else coord[1 - axis]) * NZ + cz

    class Steps:
        def __init__(self, r, axis, across_first, ending):
            self.r, self.axis, self.across_first, self.ending = r, axis, across_first, ending

        def send(self, slot, send_slot, target):
            copy = copy_of(self.r, self.axis, slot, send_slot, target)
            if self.ending:
                copy.wait_send()
            else:
                copy.start()

        def receive(self, slot):
            if not self.ending:
                copy_of(self.r, self.axis, slot, 0, z_up).wait_recv()

        def up(self, b, cz):
            @pl.when(has_up)
            def _():
                self.send(place(self.axis, b, cz), b * 5 + cz, z_up)

        def down(self, b, cz, start=False):
            @pl.when(has_down)
            def _():
                self.send(place(self.axis, b, cz), b * 5 + (NZ if start else cz), z_down)

        def across(self, cz):
            self.send(place(self.axis, 0, cz), 10 + cz, device(1 - self.axis, 1, 0))

        def begin(self):
            if self.across_first:
                self.across(z)
            self.up(0, z)
            self.down(0, z, True)
            if not self.across_first:
                self.across(z)

        def crossed(self):
            self.receive(place(self.axis, 1, z))
            self.up(1, z)
            self.down(1, z, True)

        def along(self, d, b):
            for upward in (True, False):
                cz = z - d if upward else z + d

                @pl.when(cz >= 0 if upward else cz < NZ)
                def _():
                    self.receive(place(self.axis, b, cz))
                    if d < NZ - 1:
                        (self.up if upward else self.down)(b, cz)
                    if not self.across_first:
                        self.across(cz)

    def first_round(ending):
        steps = [Steps(0, axis, True, ending) for axis in range(2)]
        if ending:
            for step in steps:
                step.begin()
        for step in steps:
            step.crossed()
        for d in range(1, NZ):
            for b in range(2):
                for step in steps:
                    step.along(d, b)

    def begin_round(r):
        for axis in range(2):
            Steps(r, axis, False, False).begin()

    def later_group(index, r):
        Steps(r, index % 2, False, False).along(1 + index // 2, 0)

    def leaves(axis, r):
        for cz in range(NZ):
            copy_of(r, axis, place(axis, 1, cz), 0, z_up).wait_recv()

    total = 2 * NZ * 4 * rows_each

    def attend(axis, r, half):
        cols = pl.ds(pl.multiple_of(r * HD, HD), HD)
        if half == 0:
            extra_buf[axis, 0:HD, :] = jnp.swapaxes(kv_buf[axis, :, 0, :, cols].reshape(total, HD), 0, 1)
        head_keys = extra_buf[axis]
        head_values = kv_buf[axis, :, 1, :, cols].reshape(total, HD)
        head_values = jnp.concatenate([head_values, jnp.ones_like(head_values)], axis=1)
        rows = 2 * q_rows
        row_block = lax.broadcasted_iota(jnp.int32, (rows, HD), 0) // BLK + half * (rows // BLK)
        chosen = (row_block == lax.broadcasted_iota(jnp.int32, (rows, HD), 1)).astype(jnp.float32).astype(jnp.bfloat16)
        sources = slice(2 * half, 2 * half + 2)
        head_queries = jnp.concatenate([q_buf[axis, sources, :, cols].reshape(rows, HD), chosen], axis=1)
        scores = jnp.dot(head_queries, head_keys, preferred_element_type=jnp.float32)
        largest = jnp.max(scores, axis=1, keepdims=True)
        raised = jnp.exp2((scores - largest) * FACTOR).astype(jnp.bfloat16)
        both = jnp.dot(raised, head_values, preferred_element_type=jnp.float32)
        done = (both[:, :HD] / both[:, HD:]).astype(jnp.bfloat16)
        o_buf[axis, sources, :, cols] = done.reshape(2, q_rows, HD)

    def out_columns(axis, r):
        start = core * HALF + axis * (HALF // 2) + coord[axis] * SERVED + r * HD
        return out_ref.at[:, pl.ds(pl.multiple_of(start, HD), HD)]

    def out_copies(axis, r):
        cols = pl.ds(pl.multiple_of(r * HD, HD), HD)
        found = []
        for p, (flip, swap) in enumerate(peers):
            a = 1 - coord[axis] if flip else coord[axis]
            c = 1 - core if swap else core
            found.append(pltpu.make_async_remote_copy(
                src_ref=o_buf.at[axis, a * 2 + c, :, cols], dst_ref=out_columns(axis, r),
                send_sem=out_send.at[r, axis, p], recv_sem=out_recv.at[r, axis, p],
                device_id=device(axis, flip, swap), device_id_type=MESH,
            ))
        return found

    def out_keep(axis, r):
        cols = pl.ds(pl.multiple_of(r * HD, HD), HD)
        return pltpu.make_async_copy(
            o_buf.at[axis, quarter(axis), :, cols], out_columns(axis, r), out_sem.at[r, axis]
        )

    def round_body(r, carry):
        @pl.when(r < ROUNDS)
        def _():
            later_group(0, r)
            later_group(1, r)

        for step in range(4):
            axis, half = step // 2, step % 2

            if half == 0:
                @pl.when(r > 1)
                def _():
                    leaves(axis, r - 1)

            attend(axis, r - 1, half)
            if half == 1:
                for copy in reversed(out_copies(axis, r - 1)):
                    copy.start()
                out_keep(axis, r - 1).start()

            if step < 2:
                @pl.when(r < ROUNDS)
                def _():
                    later_group(2 + 2 * step, r)
                    later_group(3 + 2 * step, r)

            if step == 2:
                @pl.when(r < ROUNDS - 1)
                def _():
                    begin_round(r + 1)

        return carry

    start_swaps((0, 1, 2))
    wait_swaps((0, 1))
    for axis in range(2):
        Steps(0, axis, True, False).begin()
    start_swaps((3,))
    first_round(False)
    begin_round(1)
    wait_swaps((2, 3))
    for axis in range(2):
        marks = bias_buf[axis, 0] + bias_buf[axis, 1] + bias_buf[axis, 2] + bias_buf[axis, 3]
        spread = jnp.concatenate([
            jnp.broadcast_to(marks[block:block + 1, :], (rows_each, HD))
            for slot in range(2 * NZ) for part in range(4)
            for block in [key_block(axis, slot, part, rows_each)]
        ], axis=0)
        extra_buf[axis, HD:2 * HD, :] = jnp.swapaxes(spread, 0, 1).astype(jnp.bfloat16)

    lax.fori_loop(1, ROUNDS + 1, round_body, 0)

    first_round(True)

    def end_round(r, carry):
        for axis in range(2):
            step = Steps(r, axis, False, True)
            step.begin()
            for d in range(1, NZ):
                step.along(d, 0)
        return carry

    lax.fori_loop(1, ROUNDS, end_round, 0)
    for axis in range(2):
        for p in range(3):
            for i in range(4):
                swap_copy(axis, p, i).wait_send()

    def finish(r, carry):
        for axis in range(2):
            out_keep(axis, r).wait()
            for copy in out_copies(axis, r):
                copy.wait()
        return carry

    lax.fori_loop(0, ROUNDS, finish, 0)


def gathered(queries, keys, values, key_lists, counts):
    q_rows, rows_each = queries.shape[0], keys.shape[0]
    key_total = CHIPS * 2 * rows_each
    far = pl.BlockSpec(memory_space=pltpu.HBM)
    scalars = pl.BlockSpec(memory_space=pltpu.SMEM)
    flops = 4 * 2 * q_rows * key_total * HALF
    return pl.pallas_call(
        functools.partial(gather_kernel, rows_each, q_rows),
        out_shape=jax.ShapeDtypeStruct(queries.shape, jnp.bfloat16),
        in_specs=[far] * 3 + [scalars] * 2,
        out_specs=pl.BlockSpec(memory_space=pl.ANY),
        scratch_shapes=[
            pltpu.VMEM((2, 2 * NZ, 2, 4 * rows_each, SERVED), jnp.bfloat16),
            pltpu.VMEM((2, 4, q_rows, SERVED), jnp.bfloat16),
            pltpu.VMEM((2, 4, key_total // BLK, HD), jnp.float32),
            pltpu.VMEM((2, 2 * HD, key_total), jnp.bfloat16),
            pltpu.VMEM((2, 4, q_rows, SERVED), jnp.bfloat16),
            pltpu.SemaphoreType.DMA((ROUNDS, 2, 2 * NZ)),
            pltpu.SemaphoreType.DMA((ROUNDS, 2, 14)),
            pltpu.SemaphoreType.DMA((2, 4)),
            pltpu.SemaphoreType.DMA((2, 3, 4)),
            pltpu.SemaphoreType.DMA((2, 3, 4)),
            pltpu.SemaphoreType.DMA((ROUNDS, 2)),
            pltpu.SemaphoreType.DMA((ROUNDS, 2, 3)),
            pltpu.SemaphoreType.DMA((ROUNDS, 2, 3)),
        ],
        compiler_params=pltpu.CompilerParams(
            collective_id=0, has_side_effects=True, vmem_limit_bytes=48 * 1024 * 1024
        ),
        cost_estimate=pl.CostEstimate(flops=flops, bytes_accessed=2 * queries.size * 2, transcendentals=0),
    )(queries, keys, values, key_lists, counts)


def regroup(split_array, kv_count, pb_count):
    tokens_each = split_array.shape[0] // (kv_count * pb_count)
    shaped = split_array.reshape(kv_count, pb_count, tokens_each, split_array.shape[1])
    return shaped.transpose(1, 0, 2, 3).reshape(-1, split_array.shape[1])


def per_device(queries, keys, values, key_lists, counts):
    kv_count = lax.axis_size("kv")
    pb_count = lax.axis_size("pb")
    head_local = HEADS // kv_count
    scaling = HD ** (-0.5)
    key_whole, value_whole = (
        lax.all_gather(keys, "pb", axis=0, tiled=True),
        lax.all_gather(values, "pb", axis=0, tiled=True),
    )
    key_split, value_split = (
        lax.all_to_all(key_whole, "kv", split_axis=1, concat_axis=0, tiled=True),
        lax.all_to_all(value_whole, "kv", split_axis=1, concat_axis=0, tiled=True),
    )
    key_heads = regroup(key_split, kv_count, pb_count)
    value_heads = regroup(value_split, kv_count, pb_count)
    key_blocks = key_heads.reshape(-1, BLK, head_local, HD)
    value_blocks = value_heads.reshape(-1, BLK, head_local, HD)
    slot_of_key = jnp.arange(MOST * BLK, dtype=jnp.int32) // BLK

    def padded_group(item):
        group_queries, group_lists, group_counts = item
        members = group_queries.shape[0]
        listed_keys = key_blocks[group_lists].reshape(members, MOST * BLK, head_local, HD)
        listed_values = value_blocks[group_lists].reshape(members, MOST * BLK, head_local, HD)
        scores = (
            jnp.einsum(
                "gqhd,gkhd->ghqk", group_queries, listed_keys, preferred_element_type=jnp.float32
            )
            * scaling
        )
        usable = (slot_of_key[None, :] < group_counts[:, None])[:, None, None, :]
        largest = jnp.max(jnp.where(usable, scores, -jnp.inf), axis=-1, keepdims=True)
        raised = jnp.where(usable, jnp.exp(scores - largest), 0.0)
        totals = jnp.sum(raised, axis=-1, keepdims=True)
        weights = (raised / totals).astype(jnp.bfloat16)
        output = jnp.einsum(
            "ghqk,gkhd->gqhd", weights, listed_values, preferred_element_type=jnp.float32
        )
        return output.astype(jnp.bfloat16)

    query_blocks = queries.reshape(-1, BLK, queries.shape[1])
    exchanged = lax.all_to_all(query_blocks, "kv", split_axis=2, concat_axis=0, tiled=True)
    block_total = exchanged.shape[0]
    rows = exchanged.shape[1]
    per_group = math.gcd(block_total, max(1, 512 // rows))
    group_total = block_total // per_group
    grouped = exchanged.reshape(group_total, per_group, rows, head_local, HD)
    lists_grouped = key_lists.reshape(group_total, per_group, key_lists.shape[1])
    counts_grouped = counts.reshape(group_total, per_group)
    produced = lax.map(padded_group, (grouped, lists_grouped, counts_grouped))
    joined = produced.reshape(block_total, rows, head_local * HD)
    result = lax.all_to_all(joined, "kv", split_axis=0, concat_axis=2, tiled=True)
    return result.reshape(queries.shape)


def solution(mesh):
    fits = mesh.shape["pb"] == NY * 2 and mesh.shape["kv"] == NX * NZ

    def choose(queries, keys, values, key_lists, counts):
        small = keys.shape[0] == 32 and queries.shape[0] % BLK == 0
        work = gathered if fits and small else per_device
        return work(queries, keys, values, key_lists, counts)

    return jax.shard_map(
        choose,
        mesh=mesh,
        in_specs=(
            P(("pb", "kv"), None),
            P(("pb", "kv"), None),
            P(("pb", "kv"), None),
            P("pb", None),
            P("pb"),
        ),
        out_specs=P(("pb", "kv"), None),
        check_vma=False,
    )
```

```python
import functools
import math

import jax
import jax.numpy as jnp
from jax import lax
from jax.experimental import pallas as pl
from jax.experimental.pallas import tpu as pltpu
from jax.sharding import PartitionSpec as P

HEADS = 32
HD = 128
BLK = 128
MOST = 8

NX, NY, NZ = 2, 2, 4
CHIPS = NX * NY * NZ
HALF = HEADS // 2 * HD
SERVED = HALF // 4
ROUNDS = SERVED // HD
MESH = pl.DeviceIdType.MESH
FACTOR = HD ** (-0.5) * math.log2(math.e)


def axis_coords(axis, a, b, cz):
    return (a, b, cz) if axis == 0 else (b, a, cz)


def key_block(axis, slot, quarter, rows_each):
    cx, cy, cz = axis_coords(axis, quarter // 2, slot // NZ, slot % NZ)
    return ((cy * 2 + quarter % 2) * (NZ * NX) + cz * NX + cx) * rows_each // BLK


def gather_kernel(
    rows_each, q_rows, q_ref, k_ref, v_ref, lists_ref, counts_ref, out_ref,
    kv_buf, q_buf, bias_buf, extra_buf, o_buf,
    recv_sem, send_sem, load_sem, swap_send, swap_recv, out_sem, out_send, out_recv,
):
    pb, kv = lax.axis_index("pb"), lax.axis_index("kv")
    y, core = pb // 2, pb % 2
    z, x = kv // 2, kv % 2
    coord = (x, y)

    def device(axis, flip, swap):
        cx = 1 - x if flip and axis == 0 else x
        cy = 1 - y if flip and axis == 1 else y
        return (cy * 2 + (1 - core if swap else core), z * 2 + cx)

    peers = ((0, 1), (1, 0), (1, 1))
    z_up = (pb, kv + 2)
    z_down = (pb, kv - 2)
    has_up, has_down = z < NZ - 1, z > 0

    barrier = pltpu.get_barrier_semaphore()

    def greet(target):
        pl.semaphore_signal(barrier, inc=1, device_id=target, device_id_type=MESH)

    greet(device(0, 0, 1))
    for axis in range(2):
        greet(device(axis, 1, 0))
        greet(device(axis, 1, 1))

    @pl.when(has_up)
    def _():
        greet(z_up)

    @pl.when(has_down)
    def _():
        greet(z_down)

    def heads_of(axis, flip, swap):
        c = 1 - core if swap else core
        a = 1 - coord[axis] if flip else coord[axis]
        return pl.ds(pl.multiple_of(c * HALF + axis * (HALF // 2) + a * SERVED, SERVED), SERVED)

    def quarter(axis):
        return coord[axis] * 2 + core

    def own(axis):
        return coord[1 - axis] * NZ + z

    def parts(axis, flip, swap):
        cols = heads_of(axis, flip, swap)
        mine = quarter(axis)
        tokens = pl.ds(pl.multiple_of(mine * rows_each, rows_each), rows_each)
        return [
            (k_ref.at[:, cols], kv_buf.at[axis, own(axis), 0, tokens, :]),
            (v_ref.at[:, cols], kv_buf.at[axis, own(axis), 1, tokens, :]),
            (bias_buf.at[axis, mine], bias_buf.at[axis, mine]),
            (q_ref.at[:, cols], q_buf.at[axis, mine]),
        ]

    def load(axis, i):
        source, target = parts(axis, 0, 0)[i]
        return pltpu.make_async_copy(source, target, load_sem.at[axis, i])

    def swap_copy(axis, p, i):
        source, target = parts(axis, *peers[p])[i]
        return pltpu.make_async_remote_copy(
            src_ref=source, dst_ref=target, send_sem=swap_send.at[axis, p, i], recv_sem=swap_recv.at[axis, p, i],
            device_id=device(axis, *peers[p]), device_id_type=MESH,
        )

    for i in (0, 1, 3):
        for axis in range(2):
            load(axis, i).start()

    per = q_rows // BLK
    for axis in range(2):
        tile = bias_buf.shape[2:]
        block_id = lax.broadcasted_iota(jnp.int32, tile, 0)
        lane_id = lax.broadcasted_iota(jnp.int32, tile, 1)
        tally = jnp.zeros(tile, jnp.float32)
        for one in range(per):
            row = kv * per + one
            used = counts_ref[row]
            hit = jnp.zeros(tile, jnp.float32)
            for entry in range(MOST):
                named = jnp.where(entry < used, lists_ref[row, entry], -1)
                hit = jnp.where(block_id == named, 1.0, hit)
            wanted = lane_id == quarter(axis) * per + one
            tally = jnp.where(wanted, jnp.where(hit > 0.5, 0.0, -1e30), tally)
        bias_buf[axis, quarter(axis)] = tally

    pl.semaphore_wait(barrier, 5 + has_up.astype(jnp.int32) + has_down.astype(jnp.int32))

    def start_swaps(kinds):
        for p in range(3):
            for i in kinds:
                for axis in range(2):
                    swap_copy(axis, p, i).start()

    def wait_swaps(kinds):
        for i in kinds:
            for axis in range(2):
                if i != 2:
                    load(axis, i).wait()
                for p in range(3):
                    swap_copy(axis, p, i).wait_recv()

    def copy_of(r, axis, slot, send_slot, target):
        cols = pl.ds(pl.multiple_of(r * HD, HD), HD)
        part = kv_buf.at[axis, slot, :, :, cols]
        return pltpu.make_async_remote_copy(
            src_ref=part, dst_ref=part, send_sem=send_sem.at[r, axis, send_slot],
            recv_sem=recv_sem.at[r, axis, slot], device_id=target, device_id_type=MESH,
        )

    def place(axis, b, cz):
        return (1 - coord[1 - axis] if b else coord[1 - axis]) * NZ + cz

    class Steps:
        def __init__(self, r, axis, across_first, ending):
            self.r, self.axis, self.across_first, self.ending = r, axis, across_first, ending

        def send(self, slot, send_slot, target):
            copy = copy_of(self.r, self.axis, slot, send_slot, target)
            if self.ending:
                copy.wait_send()
            else:
                copy.start()

        def receive(self, slot):
            if not self.ending:
                copy_of(self.r, self.axis, slot, 0, z_up).wait_recv()

        def up(self, b, cz):
            @pl.when(has_up)
            def _():
                self.send(place(self.axis, b, cz), b * 5 + cz, z_up)

        def down(self, b, cz, start=False):
            @pl.when(has_down)
            def _():
                self.send(place(self.axis, b, cz), b * 5 + (NZ if start else cz), z_down)

        def across(self, cz):
            self.send(place(self.axis, 0, cz), 10 + cz, device(1 - self.axis, 1, 0))

        def begin(self):
            if self.across_first:
                self.across(z)
            self.up(0, z)
            self.down(0, z, True)
            if not self.across_first:
                self.across(z)

        def crossed(self):
            self.receive(place(self.axis, 1, z))
            self.up(1, z)
            self.down(1, z, True)

        def along(self, d, b):
            for upward in (True, False):
                cz = z - d if upward else z + d

                @pl.when(cz >= 0 if upward else cz < NZ)
                def _():
                    self.receive(place(self.axis, b, cz))
                    if d < NZ - 1:
                        (self.up if upward else self.down)(b, cz)
                    if not self.across_first:
                        self.across(cz)

    def first_round(ending):
        steps = [Steps(0, axis, True, ending) for axis in range(2)]
        if ending:
            for step in steps:
                step.begin()
        for step in steps:
            step.crossed()
        for d in range(1, NZ):
            for b in range(2):
                for step in steps:
                    step.along(d, b)

    def begin_round(r):
        for axis in range(2):
            Steps(r, axis, False, False).begin()

    def later_group(index, r):
        Steps(r, index % 2, False, False).along(1 + index // 2, 0)

    def leaves(axis, r):
        for cz in range(NZ):
            copy_of(r, axis, place(axis, 1, cz), 0, z_up).wait_recv()

    total = 2 * NZ * 4 * rows_each

    def attend(axis, r, half):
        cols = pl.ds(pl.multiple_of(r * HD, HD), HD)
        if half == 0:
            extra_buf[axis, 0:HD, :] = jnp.swapaxes(kv_buf[axis, :, 0, :, cols].reshape(total, HD), 0, 1)
        head_keys = extra_buf[axis]
        head_values = kv_buf[axis, :, 1, :, cols].reshape(total, HD)
        head_values = jnp.concatenate([head_values, jnp.ones_like(head_values)], axis=1)
        rows = 2 * q_rows
        row_block = lax.broadcasted_iota(jnp.int32, (rows, HD), 0) // BLK + half * (rows // BLK)
        chosen = (row_block == lax.broadcasted_iota(jnp.int32, (rows, HD), 1)).astype(jnp.float32).astype(jnp.bfloat16)
        sources = slice(2 * half, 2 * half + 2)
        head_queries = jnp.concatenate([q_buf[axis, sources, :, cols].reshape(rows, HD), chosen], axis=1)
        scores = jnp.dot(head_queries, head_keys, preferred_element_type=jnp.float32)
        largest = jnp.max(scores, axis=1, keepdims=True)
        raised = jnp.exp2((scores - largest) * FACTOR).astype(jnp.bfloat16)
        both = jnp.dot(raised, head_values, preferred_element_type=jnp.float32)
        done = (both[:, :HD] / both[:, HD:]).astype(jnp.bfloat16)
        o_buf[axis, sources, :, cols] = done.reshape(2, q_rows, HD)

    def out_columns(axis, r):
        start = core * HALF + axis * (HALF // 2) + coord[axis] * SERVED + r * HD
        return out_ref.at[:, pl.ds(pl.multiple_of(start, HD), HD)]

    def out_copies(axis, r):
        cols = pl.ds(pl.multiple_of(r * HD, HD), HD)
        found = []
        for p, (flip, swap) in enumerate(peers):
            a = 1 - coord[axis] if flip else coord[axis]
            c = 1 - core if swap else core
            found.append(pltpu.make_async_remote_copy(
                src_ref=o_buf.at[axis, a * 2 + c, :, cols], dst_ref=out_columns(axis, r),
                send_sem=out_send.at[r, axis, p], recv_sem=out_recv.at[r, axis, p],
                device_id=device(axis, flip, swap), device_id_type=MESH,
            ))
        return found

    def out_keep(axis, r):
        cols = pl.ds(pl.multiple_of(r * HD, HD), HD)
        return pltpu.make_async_copy(
            o_buf.at[axis, quarter(axis), :, cols], out_columns(axis, r), out_sem.at[r, axis]
        )

    def round_body(r, carry):
        @pl.when(r < ROUNDS - 1)
        def _():
            begin_round(r + 1)

        @pl.when(r < ROUNDS)
        def _():
            later_group(0, r)
            later_group(1, r)

        for step in range(4):
            axis, half = step // 2, step % 2

            if half == 0:
                @pl.when(r > 1)
                def _():
                    leaves(axis, r - 1)

            attend(axis, r - 1, half)
            if half == 1:
                for copy in reversed(out_copies(axis, r - 1)):
                    copy.start()
                out_keep(axis, r - 1).start()

            if step < 2:
                @pl.when(r < ROUNDS)
                def _():
                    later_group(2 + 2 * step, r)
                    later_group(3 + 2 * step, r)

        return carry

    start_swaps((0, 1, 2))
    wait_swaps((0, 1))
    for axis in range(2):
        Steps(0, axis, True, False).begin()
    start_swaps((3,))
    begin_round(1)
    first_round(False)
    wait_swaps((2, 3))
    for axis in range(2):
        marks = bias_buf[axis, 0] + bias_buf[axis, 1] + bias_buf[axis, 2] + bias_buf[axis, 3]
        spread = jnp.concatenate([
            jnp.broadcast_to(marks[block:block + 1, :], (rows_each, HD))
            for slot in range(2 * NZ) for part in range(4)
            for block in [key_block(axis, slot, part, rows_each)]
        ], axis=0)
        extra_buf[axis, HD:2 * HD, :] = jnp.swapaxes(spread, 0, 1).astype(jnp.bfloat16)

    lax.fori_loop(1, ROUNDS + 1, round_body, 0)

    first_round(True)

    def end_round(r, carry):
        for axis in range(2):
            step = Steps(r, axis, False, True)
            step.begin()
            for d in range(1, NZ):
                step.along(d, 0)
        return carry

    lax.fori_loop(1, ROUNDS, end_round, 0)
    for axis in range(2):
        for p in range(3):
            for i in range(4):
                swap_copy(axis, p, i).wait_send()

    def finish(r, carry):
        for axis in range(2):
            out_keep(axis, r).wait()
            for copy in out_copies(axis, r):
                copy.wait()
        return carry

    lax.fori_loop(0, ROUNDS, finish, 0)


def gathered(queries, keys, values, key_lists, counts):
    q_rows, rows_each = queries.shape[0], keys.shape[0]
    key_total = CHIPS * 2 * rows_each
    far = pl.BlockSpec(memory_space=pltpu.HBM)
    scalars = pl.BlockSpec(memory_space=pltpu.SMEM)
    flops = 4 * 2 * q_rows * key_total * HALF
    return pl.pallas_call(
        functools.partial(gather_kernel, rows_each, q_rows),
        out_shape=jax.ShapeDtypeStruct(queries.shape, jnp.bfloat16),
        in_specs=[far] * 3 + [scalars] * 2,
        out_specs=pl.BlockSpec(memory_space=pl.ANY),
        scratch_shapes=[
            pltpu.VMEM((2, 2 * NZ, 2, 4 * rows_each, SERVED), jnp.bfloat16),
            pltpu.VMEM((2, 4, q_rows, SERVED), jnp.bfloat16),
            pltpu.VMEM((2, 4, key_total // BLK, HD), jnp.float32),
            pltpu.VMEM((2, 2 * HD, key_total), jnp.bfloat16),
            pltpu.VMEM((2, 4, q_rows, SERVED), jnp.bfloat16),
            pltpu.SemaphoreType.DMA((ROUNDS, 2, 2 * NZ)),
            pltpu.SemaphoreType.DMA((ROUNDS, 2, 14)),
            pltpu.SemaphoreType.DMA((2, 4)),
            pltpu.SemaphoreType.DMA((2, 3, 4)),
            pltpu.SemaphoreType.DMA((2, 3, 4)),
            pltpu.SemaphoreType.DMA((ROUNDS, 2)),
            pltpu.SemaphoreType.DMA((ROUNDS, 2, 3)),
            pltpu.SemaphoreType.DMA((ROUNDS, 2, 3)),
        ],
        compiler_params=pltpu.CompilerParams(
            collective_id=0, has_side_effects=True, vmem_limit_bytes=61 * 1024 * 1024
        ),
        cost_estimate=pl.CostEstimate(flops=flops, bytes_accessed=2 * queries.size * 2, transcendentals=0),
    )(queries, keys, values, key_lists, counts)


def regroup(split_array, kv_count, pb_count):
    tokens_each = split_array.shape[0] // (kv_count * pb_count)
    shaped = split_array.reshape(kv_count, pb_count, tokens_each, split_array.shape[1])
    return shaped.transpose(1, 0, 2, 3).reshape(-1, split_array.shape[1])


def per_device(queries, keys, values, key_lists, counts):
    kv_count = lax.axis_size("kv")
    pb_count = lax.axis_size("pb")
    head_local = HEADS // kv_count
    scaling = HD ** (-0.5)
    key_whole, value_whole = (
        lax.all_gather(keys, "pb", axis=0, tiled=True),
        lax.all_gather(values, "pb", axis=0, tiled=True),
    )
    key_split, value_split = (
        lax.all_to_all(key_whole, "kv", split_axis=1, concat_axis=0, tiled=True),
        lax.all_to_all(value_whole, "kv", split_axis=1, concat_axis=0, tiled=True),
    )
    key_heads = regroup(key_split, kv_count, pb_count)
    value_heads = regroup(value_split, kv_count, pb_count)
    key_blocks = key_heads.reshape(-1, BLK, head_local, HD)
    value_blocks = value_heads.reshape(-1, BLK, head_local, HD)
    slot_of_key = jnp.arange(MOST * BLK, dtype=jnp.int32) // BLK

    def padded_group(item):
        group_queries, group_lists, group_counts = item
        members = group_queries.shape[0]
        listed_keys = key_blocks[group_lists].reshape(members, MOST * BLK, head_local, HD)
        listed_values = value_blocks[group_lists].reshape(members, MOST * BLK, head_local, HD)
        scores = (
            jnp.einsum(
                "gqhd,gkhd->ghqk", group_queries, listed_keys, preferred_element_type=jnp.float32
            )
            * scaling
        )
        usable = (slot_of_key[None, :] < group_counts[:, None])[:, None, None, :]
        largest = jnp.max(jnp.where(usable, scores, -jnp.inf), axis=-1, keepdims=True)
        raised = jnp.where(usable, jnp.exp(scores - largest), 0.0)
        totals = jnp.sum(raised, axis=-1, keepdims=True)
        weights = (raised / totals).astype(jnp.bfloat16)
        output = jnp.einsum(
            "ghqk,gkhd->gqhd", weights, listed_values, preferred_element_type=jnp.float32
        )
        return output.astype(jnp.bfloat16)

    query_blocks = queries.reshape(-1, BLK, queries.shape[1])
    exchanged = lax.all_to_all(query_blocks, "kv", split_axis=2, concat_axis=0, tiled=True)
    block_total = exchanged.shape[0]
    rows = exchanged.shape[1]
    per_group = math.gcd(block_total, max(1, 512 // rows))
    group_total = block_total // per_group
    grouped = exchanged.reshape(group_total, per_group, rows, head_local, HD)
    lists_grouped = key_lists.reshape(group_total, per_group, key_lists.shape[1])
    counts_grouped = counts.reshape(group_total, per_group)
    produced = lax.map(padded_group, (grouped, lists_grouped, counts_grouped))
    joined = produced.reshape(block_total, rows, head_local * HD)
    result = lax.all_to_all(joined, "kv", split_axis=0, concat_axis=2, tiled=True)
    return result.reshape(queries.shape)


def solution(mesh):
    fits = mesh.shape["pb"] == NY * 2 and mesh.shape["kv"] == NX * NZ

    def choose(queries, keys, values, key_lists, counts):
        small = keys.shape[0] == 32 and queries.shape[0] % BLK == 0
        work = gathered if fits and small else per_device
        return work(queries, keys, values, key_lists, counts)

    return jax.shard_map(
        choose,
        mesh=mesh,
        in_specs=(
            P(("pb", "kv"), None),
            P(("pb", "kv"), None),
            P(("pb", "kv"), None),
            P("pb", None),
            P("pb"),
        ),
        out_specs=P(("pb", "kv"), None),
        check_vma=False,
    )
```
